32 devices in a mesh: parts: 2 (over x), space: 16 (over z, y, core).
Axes of the slice: x: 2, y: 2, z: 4, core: 2. Of those that a mesh axis runs over, the one named last changes fastest.
Arguments:
- vectors: bfloat16 [2, 12, 4, 3, 32, 8, 128], P(None, None, None, None, ('parts', 'space')), parts along dimension 4, may hold values from -6 to 6
- links: bfloat16 [2, 4, 3, 3, 32, 8, 128], P(None, None, None, None, ('parts', 'space')), parts along dimension 4, may hold values from -6 to 6
- clover: bfloat16 [2, 2, 6, 6, 32, 8, 128], P(None, None, None, None, ('parts', 'space')), parts along dimension 4, may hold values from -4 to 4
- block_owner: int32 [4096, 1], P(('parts', 'space')), parts along dimension 0, may hold values from 0 to 15; in each aligned block of 128 rows (0 to 127, 128 to 255, ...) at most 16 rows name the same one
- block_aggregate: int32 [4096], P(('parts', 'space')), parts along dimension 0, may hold values from 0 to 3
Outputs:
- applied: bfloat16 [2, 12, 4, 3, 32, 8, 128], P(None, None, None, None, ('parts', 'space')), parts along dimension 4
- coarse: float32 [128, 2, 12, 12], P(('parts', 'space')), parts along dimension 0
The draws below stay inside these ranges and needn't reach their ends.
There are 2 independent parts, one for each index of `parts`. The reference program is written for one: setup_inputs(seed, part) draws one part's arguments, and reference() takes and returns one part's arrays. A program takes and returns all parts, laid end to end along the dimension named above; each array names one. Nothing has to cross between parts.
Inputs may be any that keep to these rules, and one draw needn't show every extreme that they name: `block_owner`: the 128 blocks of one device name one owner at most 16 times, and in every draw some device names some owner exactly 16 times.
All inputs are finite; a program needn't handle non-finite values.
Results may differ from the reference program's by a relative error of at most 0.003.
Values may be sent and summed in bfloat16 or wider, within the bound.
A program may use at most 192 MiB of HBM per device.

```python
import math
import jax
import jax.numpy as jnp
import numpy as np
from jax import lax

VECTORS = 12
CX = 1
CY = 8
CZ = 8
CT = 16
AGG_DEV = 4
LX = 16
ZT = 128
BLOCKS_DEV = 128
BLOCK_SITES = 8
BLOCKS = 2048
AGG = 64
CAP = 16
N_SPACE = 16


def touch_ends(result, own_key, smallest, largest):
    extent = result.shape
    index_at = [jax.random.randint(jax.random.fold_in(own_key, axis), (), 0, extent[axis]) for axis in range(len(extent))]
    result = result.at[tuple(index_at)].set(smallest)
    longest = extent.index(max(extent))
    index_at[longest] = (index_at[longest] + 1) % extent[longest]
    return result.at[tuple(index_at)].set(largest)


def block_levels(stream_key, extent, cuts, smallest, largest):
    level, own = 1.0, jax.random.fold_in(stream_key, 6)
    for position, parts in cuts:
        draws = jnp.exp(jax.random.uniform(jax.random.fold_in(own, position), (parts,), jnp.float32, smallest / len(cuts), largest / len(cuts)))
        level = level * jnp.repeat(draws, extent[position] // parts).reshape([-1 if axis == position else 1 for axis in range(len(extent))])
    return level


def deal_out(key, own, number, rows, number_of, top, limit, lean):
    sequence = jax.random.permutation(key, number_of)
    packed, common = portions_of(number_of, rows * top, limit, lean, True), portions_of(number_of, rows * top, limit, lean, False)
    places = jnp.arange(number_of)

    def named(tallies, rotation):
        used = int((tallies > 0).sum())
        fixed = max(1, used // 4)
        shifted = fixed + (places - fixed + rotation * (used - fixed)) % max(1, number_of - fixed)
        return jnp.zeros((number_of,), jnp.int32).at[sequence[jnp.where(places < fixed, places, shifted)]].set(jnp.asarray(tallies, jnp.int32))

    tallies = jnp.where(number % 4 == 0, named(packed, number // 4), named(common, number - number // 4 - 1))
    mixed = jax.random.permutation(jax.random.fold_in(own, 3), number_of)
    giver, receiver = mixed[0:number_of // 2 * 2:2], mixed[1:number_of // 2 * 2:2]
    margin = jnp.minimum(tallies[giver] - 1, limit - tallies[receiver]) // 2
    margin = jnp.where((giver == sequence[0]) | (receiver == sequence[0]) | (tallies[receiver] == 0), 0, jnp.maximum(margin, 0))
    shifted = jax.random.randint(jax.random.fold_in(own, 4), (number_of // 2,), 0, 1 << 20) % (margin + 1)
    tallies = tallies.at[giver].add(-shifted).at[receiver].add(shifted)
    members = jnp.searchsorted(jnp.cumsum(tallies), jnp.arange(rows * top), side="right").astype(jnp.int32)
    table = members.reshape(top, rows).T
    table = table[jax.random.permutation(jax.random.fold_in(own, 1), rows)]
    rotation = jax.random.randint(jax.random.fold_in(own, 2), (rows, 1), 0, top)
    return jnp.take_along_axis(table, (jnp.arange(top)[None, :] + rotation) % top, axis=1)


def portions_of(number_of, total, bound, lean, full):
    portions = [(1 << 20) // math.isqrt(rank ** lean) + 1 for rank in range(1, number_of + 1)]
    largest = bound if full else min(bound, max(-(-total // number_of), total * portions[0] // sum(portions)))
    least = 1 if total - largest >= number_of - 1 else 0
    holding, rest = [largest] + [least] * (number_of - 1), total - largest - least * (number_of - 1)
    while rest > 0:
        movable = [i for i in range(1, number_of) if holding[i] < largest] or [i for i in range(1, number_of) if holding[i] < bound]
        pool, left = sum([portions[i] for i in movable]), rest
        for i in movable:
            more = min(bound - holding[i], max(1, left * portions[i] // pool), rest)
            holding[i] = holding[i] + more
            rest = rest - more
    return np.array(holding)


def centred(stream_key, dims, deviation, bound, pieces=(), kind=jnp.bfloat16):
    drawn = deviation * jax.random.normal(stream_key, dims, jnp.float32)
    if pieces:
        drawn = drawn * block_levels(stream_key, dims, pieces, -0.22, 0.18)
    return jnp.clip(drawn, -bound, bound).astype(kind)


def setup_inputs(seed: int = 0, part: int = 0) -> dict:
    keys = jax.random.split(jax.random.key(seed), 6)
    part_splits = jax.random.split(jax.random.fold_in(keys[5], part), 6)
    vectors = centred(part_splits[0], (2, VECTORS, 4, 3, LX, CY, ZT), 1.0, 6.0, ((4, 16),))
    links = centred(part_splits[1], (2, 4, 3, 3, LX, CY, ZT), 0.4, 6.0, ((4, 16),))
    clover = centred(part_splits[2], (2, 2, 6, 6, LX, CY, ZT), 0.25, 4.0, ((4, 16),))
    block_owner_keys = jax.random.split(jax.random.fold_in(part_splits[3], 1), BLOCKS // BLOCKS_DEV)
    block_owner_turns = jax.random.permutation(jax.random.fold_in(part_splits[3], 3), BLOCKS // BLOCKS_DEV)
    block_owner = jax.vmap(lambda own, number: deal_out(jax.random.fold_in(part_splits[3], 2), own, number, BLOCKS_DEV, N_SPACE, 1, CAP, 2))(block_owner_keys, block_owner_turns).reshape((BLOCKS, 1))
    block_aggregate = touch_ends(jax.random.randint(part_splits[4], (BLOCKS,), 0, AGG_DEV), jax.random.fold_in(part_splits[4], 1), 0, AGG_DEV - 1).astype(jnp.int32)
    return dict(vectors=vectors, links=links, clover=clover, block_owner=block_owner, block_aggregate=block_aggregate)


def block_four(upper_left, upper_right, lower_left, lower_right):
    rows = [list(upper_left[i]) + list(upper_right[i]) for i in range(2)]
    rows = rows + [list(lower_left[i]) + list(lower_right[i]) for i in range(2)]
    return np.array(rows, dtype=complex)


def two_on_two(upper, lower):
    rows = [list(upper[i]) for i in range(2)] + [list(lower[i]) for i in range(2)]
    return np.array(rows, dtype=complex)


def spin_tables():
    pauli_list = [np.array([[0, 1], [1, 0]], dtype=complex), np.array([[0, -1j], [1j, 0]], dtype=complex), np.array([[1, 0], [0, -1]], dtype=complex)]
    zeros_two = np.zeros((2, 2), dtype=complex)
    ident_two = np.eye(2, dtype=complex)
    gammas = [block_four(zeros_two, -1j * pauli, 1j * pauli, zeros_two) for pauli in pauli_list]
    gammas.append(block_four(zeros_two, ident_two, ident_two, zeros_two))
    minus_proj = np.stack([(np.eye(4) - gamma)[:2, :] for gamma in gammas])
    plus_proj = np.stack([(np.eye(4) + gamma)[:2, :] for gamma in gammas])
    minus_back = np.stack([two_on_two(ident_two, -gamma[2:, :2]) for gamma in gammas])
    plus_back = np.stack([two_on_two(ident_two, gamma[2:, :2]) for gamma in gammas])
    tables = []
    for table in (minus_proj, plus_proj, minus_back, plus_back):
        tables.append((table.real.astype(np.float32), table.imag.astype(np.float32)))
    return tables


def contract(form, left, right):
    return jnp.einsum(form, left, right, precision=lax.Precision.HIGHEST)


def color_apply(link_real, link_imag, field_real, field_imag, dagger):
    if dagger:
        form = "baxyz,...sbxyz->...saxyz"
        twisted_imag = -link_imag
    else:
        form = "abxyz,...sbxyz->...saxyz"
        twisted_imag = link_imag
    out_real = contract(form, link_real, field_real) - contract(form, twisted_imag, field_imag)
    out_imag = contract(form, link_real, field_imag) + contract(form, twisted_imag, field_real)
    return out_real, out_imag


def spin_apply(table_real, table_imag, field_real, field_imag):
    form = "st,...taxyz->...saxyz"
    table_real = jnp.asarray(table_real)
    table_imag = jnp.asarray(table_imag)
    out_real = contract(form, table_real, field_real) - contract(form, table_imag, field_imag)
    out_imag = contract(form, table_real, field_imag) + contract(form, table_imag, field_real)
    return out_real, out_imag


def to_half(real_part, imag_part):
    stacked = jnp.stack([real_part, imag_part]).astype(jnp.bfloat16)
    stacked = lax.optimization_barrier(stacked)
    wide = stacked.astype(jnp.float32)
    return wide[0], wide[1]


def lower_half(direction, field_real, field_imag):
    tables = spin_tables()
    proj_real, proj_imag = tables[0]
    out_real, out_imag = spin_apply(proj_real[direction], proj_imag[direction], field_real, field_imag)
    return to_half(out_real, out_imag)


def upper_half(direction, link_real, link_imag, field_real, field_imag):
    tables = spin_tables()
    proj_real, proj_imag = tables[1]
    out_real, out_imag = spin_apply(proj_real[direction], proj_imag[direction], field_real, field_imag)
    out_real, out_imag = color_apply(link_real, link_imag, out_real, out_imag, True)
    return to_half(out_real, out_imag)


def move(field, direction, step, twisted):
    if direction == 1:
        return jnp.roll(field, -step, axis=-2)
    shape = field.shape
    split = field.reshape(shape[:-1] + (CZ, CT))
    if direction == 2:
        rolled = jnp.roll(split, -step, axis=-2)
    else:
        rolled = jnp.roll(split, -step, axis=-1)
        if twisted:
            times = jnp.arange(CT)
            edge = CT - 1 if step > 0 else 0
            rolled = jnp.where(times == edge, -rolled, rolled)
    return rolled.reshape(shape)


def clover_apply(clover_real, clover_imag, field_real, field_imag):
    shape = field_real.shape
    paired = shape[:-5] + (2, 6) + shape[-3:]
    form = "hijxyz,...hjxyz->...hixyz"
    left_real = field_real.reshape(paired)
    left_imag = field_imag.reshape(paired)
    out_real = contract(form, clover_real, left_real) - contract(form, clover_imag, left_imag)
    out_imag = contract(form, clover_real, left_imag) + contract(form, clover_imag, left_real)
    return out_real.reshape(shape), out_imag.reshape(shape)


def operator(field_real, field_imag, links_real, links_imag, clover_real, clover_imag, ahead_x, behind_x):
    tables = spin_tables()
    minus_real, minus_imag = tables[2]
    plus_real, plus_imag = tables[3]
    local_real, local_imag = clover_apply(clover_real, clover_imag, field_real, field_imag)
    total_real = 4.0 * field_real + local_real
    total_imag = 4.0 * field_imag + local_imag
    for direction in range(4):
        if direction == 0:
            ahead = ahead_x
            behind = behind_x
        else:
            lowered = lower_half(direction, field_real, field_imag)
            raised = upper_half(direction, links_real[direction], links_imag[direction], field_real, field_imag)
            ahead = (move(lowered[0], direction, 1, True), move(lowered[1], direction, 1, True))
            behind = (move(raised[0], direction, -1, True), move(raised[1], direction, -1, True))
        forward = color_apply(links_real[direction], links_imag[direction], ahead[0], ahead[1], False)
        forward = spin_apply(minus_real[direction], minus_imag[direction], forward[0], forward[1])
        backward = spin_apply(plus_real[direction], plus_imag[direction], behind[0], behind[1])
        total_real = total_real - 0.5 * (forward[0] + backward[0])
        total_imag = total_imag - 0.5 * (forward[1] + backward[1])
    return total_real, total_imag


def block_sums(vector_part, applied_part):
    form = "ksaxyn,jsaxyn->kjn"
    left_real = vector_part[0].astype(jnp.float32)
    left_imag = vector_part[1].astype(jnp.float32)
    right_real = applied_part[0].astype(jnp.float32)
    right_imag = applied_part[1].astype(jnp.float32)
    sum_real = contract(form, left_real, right_real) + contract(form, left_imag, right_imag)
    sum_imag = contract(form, left_real, right_imag) - contract(form, left_imag, right_real)
    return jnp.stack([sum_real, sum_imag])


def reference(vectors, links, clover, block_owner, block_aggregate):
    links_wide = links.astype(jnp.float32)
    clover_wide = clover.astype(jnp.float32)
    links_real = links_wide[0]
    links_imag = links_wide[1]

    def one_vector(single):
        field_real = single[0].astype(jnp.float32)
        field_imag = single[1].astype(jnp.float32)
        lowered = lower_half(0, field_real, field_imag)
        raised = upper_half(0, links_real[0], links_imag[0], field_real, field_imag)
        ahead_x = (jnp.roll(lowered[0], -1, axis=-3), jnp.roll(lowered[1], -1, axis=-3))
        behind_x = (jnp.roll(raised[0], 1, axis=-3), jnp.roll(raised[1], 1, axis=-3))
        out_real, out_imag = operator(field_real, field_imag, links_real, links_imag, clover_wide[0], clover_wide[1], ahead_x, behind_x)
        return jnp.stack([out_real, out_imag]).astype(jnp.bfloat16)

    applied_major = lax.map(one_vector, jnp.moveaxis(vectors, 1, 0))
    applied = jnp.moveaxis(applied_major, 0, 1)
    split_shape = (2, VECTORS, 4, 3, N_SPACE, CX, CY, ZT)
    vector_blocks = jnp.moveaxis(vectors.reshape(split_shape), 4, 0)
    applied_blocks = jnp.moveaxis(applied.reshape(split_shape), 4, 0)
    partial_value = lax.map(lambda pair: block_sums(pair[0], pair[1]), (vector_blocks, applied_blocks))
    partial_value = jnp.transpose(partial_value, (0, 4, 1, 2, 3)).reshape(BLOCKS, 2 * VECTORS * VECTORS)
    targets = (block_owner[:, 0] * AGG_DEV + block_aggregate).astype(jnp.int32)
    summed = jax.ops.segment_sum(partial_value, targets, num_segments=AGG)
    coarse = summed / (12.0 * BLOCK_SITES)
    return applied, coarse.reshape(AGG, 2, VECTORS, VECTORS)
```

```python
import functools
import jax
import jax.numpy as jnp
from jax import lax
from jax.experimental import pallas as pl
from jax.experimental.pallas import tpu as pltpu
from jax.sharding import PartitionSpec as P

VECTORS = 12
CT = 16
AGG_DEV = 4
BLOCK_SITES = 8
CHUNK = 3
CHUNKS = VECTORS // CHUNK
LANES = 256
MESH = pl.DeviceIdType.MESH
F32 = jnp.float32
BF16 = jnp.bfloat16

BACK = (
    ((1, (0, 1)), (0, (0, 1))),
    ((1, (1, 0)), (0, (-1, 0))),
    ((0, (0, 1)), (1, (0, -1))),
    ((0, (1, 0)), (1, (1, 0))),
)


def plus(base, factor, value):
    real, imag = factor
    if real:
        if real > 0:
            return (base[0] + value[0], base[1] + value[1])
        return (base[0] - value[0], base[1] - value[1])
    if imag > 0:
        return (base[0] - value[1], base[1] + value[0])
    return (base[0] + value[1], base[1] - value[0])


def flip(factor):
    return (-factor[0], -factor[1])


def project(mu, sign, field):
    out = []
    for row in range(2):
        column, factor = BACK[mu][row]
        if (sign > 0) != (mu == 3):
            factor = flip(factor)
        out.append([plus(field[row][a], factor, field[2 + column][a]) for a in range(3)])
    return out


def rebuild(mu, sign, total, half):
    for row in range(2):
        for a in range(3):
            total[row][a] = plus(total[row][a], (1, 0), half[row][a])
        column, factor = BACK[mu][row]
        if sign < 0:
            factor = flip(factor)
        for a in range(3):
            total[2 + row][a] = plus(total[2 + row][a], factor, half[column][a])
    return total


def color(link, dagger, half):
    out = []
    for row in half:
        line = []
        for a in range(3):
            real = imag = None
            for b in range(3):
                fr, fi = row[b]
                if dagger:
                    ur, ui = link(b, a)
                    r, i = ur * fr + ui * fi, ur * fi - ui * fr
                else:
                    ur, ui = link(a, b)
                    r, i = ur * fr - ui * fi, ur * fi + ui * fr
                real = r if real is None else real + r
                imag = i if imag is None else imag + i
            line.append((real, imag))
        out.append(line)
    return out


def rounded(half):
    flat = [part for row in half for pair in row for part in pair]
    flat = [part.astype(BF16).astype(F32) for part in flat]
    return unflatten(flat)


def unflatten(flat):
    return [[(flat[(s * 3 + a) * 2], flat[(s * 3 + a) * 2 + 1]) for a in range(3)] for s in range(len(flat) // 6)]


def mapped(half, function):
    return [[(function(p[0]), function(p[1])) for p in row] for row in half]


def rows_of(block, count):
    return [block[8 * i : 8 * i + 8] for i in range(count)]


def gathered(values, level=4):
    if len(values) == 1:
        return values[0]
    low = (lax.broadcasted_iota(jnp.int32, values[0].shape, 0) & level) == 0
    half = len(values) // 2
    out = []
    for i in range(half):
        a, b = values[i], values[i + half]
        kept = jnp.where(low, a, b)
        other = jnp.where(low, b, a)
        if level == 4:
            moved = pltpu.roll(other, 4, axis=0)
        else:
            moved = jnp.where(low, pltpu.roll(other, 8 - level, axis=0), pltpu.roll(other, level, axis=0))
        out.append(kept + moved)
    return gathered(out, level // 2)


def kernel(
    n_space, v_ref, u_ref, c_ref, owner_ref, agg_ref, applied_ref, coarse_ref,
    vf, uf, cf, acc, low_out, high_out, low_in, high_in, pairs, terms_out, terms_in,
    low_send, low_recv, high_send, high_recv, term_send, term_recv,
):
    part = lax.axis_index("parts")
    me = lax.axis_index("space")
    above = lax.rem(me + 1, n_space)
    below = lax.rem(me + n_space - 1, n_space)
    barrier = pltpu.get_barrier_semaphore()

    @pl.loop(1, n_space)
    def _(step):
        peer = lax.rem(me + step, n_space)
        pl.semaphore_signal(barrier, inc=1, device_id=(part, peer), device_id_type=MESH)

    lanes = lax.broadcasted_iota(jnp.int32, (8, 128), 1)
    last_time = (lanes & (CT - 1)) == CT - 1
    first_time = (lanes & (CT - 1)) == 0

    for c in range(2):
        for i in range(18):
            for j, block in enumerate(rows_of(u_ref[c, 16 * i : 16 * i + 16, :].astype(F32), 2)):
                at = 2 * i + j
                if at >= 27:
                    block = jnp.where(last_time, -block, block)
                uf[c, at] = block

    def link(mu):
        return lambda a, b: (uf[0, mu * 9 + a * 3 + b], uf[1, mu * 9 + a * 3 + b])

    def field_of(k):
        return [[(vf[0, k, s * 3 + a], vf[1, k, s * 3 + a]) for a in range(3)] for s in range(4)]

    def put_half(ref, k, half):
        flat = [half[s][a][c] for c in range(2) for s in range(2) for a in range(3)]
        for i in range(6):
            both = jnp.concatenate([flat[2 * i], flat[2 * i + 1]], axis=0)
            ref[k, 16 * i : 16 * i + 16, :] = both.astype(BF16)

    def get_half(ref, k):
        flat = []
        for i in range(6):
            flat += rows_of(ref[k, 16 * i : 16 * i + 16, :].astype(F32), 2)
        return [[(flat[s * 3 + a], flat[6 + s * 3 + a]) for a in range(3)] for s in range(2)]

    def halo(chunk):
        at = pl.ds(chunk * CHUNK, CHUNK)
        down = pltpu.make_async_remote_copy(
            src_ref=low_out.at[at], dst_ref=low_in.at[at],
            send_sem=low_send.at[chunk], recv_sem=low_recv.at[chunk],
            device_id=(part, below), device_id_type=MESH)
        up = pltpu.make_async_remote_copy(
            src_ref=high_out.at[at], dst_ref=high_in.at[at],
            send_sem=high_send.at[chunk], recv_sem=high_recv.at[chunk],
            device_id=(part, above), device_id_type=MESH)
        return down, up

    def first(k):
        for c in range(2):
            for i in range(6):
                for j, block in enumerate(rows_of(v_ref[c, k, 16 * i : 16 * i + 16, :].astype(F32), 2)):
                    vf[c, k, 2 * i + j] = block
        field = field_of(k)
        put_half(low_out, k, project(0, -1, field))
        put_half(high_out, k, color(link(0), True, project(0, 1, field)))

    def first_chunk(chunk):
        @pl.loop(0, CHUNK)
        def _(i):
            first(chunk * CHUNK + i)

    for chunk in range(CHUNKS):
        first_chunk(chunk)
        if chunk == 0:
            pl.semaphore_wait(barrier, n_space - 1)
        for copy in halo(chunk):
            copy.start()

    for c in range(2):
        for i in range(36):
            for j, block in enumerate(rows_of(c_ref[c, 16 * i : 16 * i + 16, :].astype(F32), 2)):
                cf[c, 2 * i + j] = block

    def ahead(mu, x):
        if mu == 1:
            return pltpu.roll(x, 7, axis=0)
        if mu == 2:
            return pltpu.roll(x, 128 - CT, axis=1)
        return jnp.where(last_time, pltpu.roll(x, CT - 1, axis=1), pltpu.roll(x, 127, axis=1))

    def behind(mu, x):
        if mu == 1:
            return pltpu.roll(x, 1, axis=0)
        if mu == 2:
            return pltpu.roll(x, CT, axis=1)
        return jnp.where(first_time, pltpu.roll(x, 128 - CT + 1, axis=1), pltpu.roll(x, 1, axis=1))

    @pl.loop(0, VECTORS)
    def _(k):
        total = None
        for mu in range(1, 4):
            field = field_of(k)
            lowered = mapped(rounded(project(mu, -1, field)), functools.partial(ahead, mu))
            forward = color(link(mu), False, lowered)
            raised = rounded(color(link(mu), True, project(mu, 1, field)))
            backward = mapped(raised, functools.partial(behind, mu))
            if total is None:
                zero = jnp.zeros((8, 128), F32)
                total = [[(zero, zero) for _ in range(3)] for _ in range(4)]
            total = rebuild(mu, -1, total, forward)
            total = rebuild(mu, 1, total, backward)
        field = field_of(k)
        for h in range(2):
            for row in range(6):
                real = imag = None
                for column in range(6):
                    at = h * 36 + row * 6 + column
                    cr, ci = cf[0, at], cf[1, at]
                    fr, fi = field[2 * h + column // 3][column % 3]
                    r, i = cr * fr - ci * fi, cr * fi + ci * fr
                    real = r if real is None else real + r
                    imag = i if imag is None else imag + i
                s, a = 2 * h + row // 3, row % 3
                fr, fi = field[s][a]
                tr, ti = total[s][a]
                acc[0, k, s * 3 + a] = 4.0 * fr + real - 0.5 * tr
                acc[1, k, s * 3 + a] = 4.0 * fi + imag - 0.5 * ti

    def finish(j):
        forward = color(link(0), False, get_half(low_in, j))
        backward = get_half(high_in, j)
        zero = jnp.zeros((8, 128), F32)
        total = [[(zero, zero) for _ in range(3)] for _ in range(4)]
        total = rebuild(0, -1, total, forward)
        total = rebuild(0, 1, total, backward)
        right = [[], []]
        for c in range(2):
            for i in range(6):
                both = []
                for at in (2 * i, 2 * i + 1):
                    both.append(acc[c, j, at] - 0.5 * total[at // 3][at % 3][c])
                both = jnp.concatenate(both, axis=0).astype(BF16)
                applied_ref[c, j, 16 * i : 16 * i + 16, :] = both
                right[c] += rows_of(both.astype(F32), 2)
        sums = [[], []]
        for k in range(VECTORS):
            real = imag = None
            for at in range(12):
                vr, vi = vf[0, k, at], vf[1, k, at]
                ar, ai = right[0][at], right[1][at]
                r, i = vr * ar + vi * ai, vr * ai - vi * ar
                real = r if real is None else real + r
                imag = i if imag is None else imag + i
            sums[0].append(real)
            sums[1].append(imag)
        flat = sums[0] + sums[1]
        for g in range(3):
            pairs[j, 8 * g : 8 * g + 8, :] = gathered(flat[8 * g : 8 * g + 8])

    for chunk in range(CHUNKS):
        for copy in halo(chunk):
            copy.wait_recv()

        @pl.loop(0, CHUNK)
        def _(i, chunk=chunk):
            finish(chunk * CHUNK + i)

    targets = owner_ref[...] * AGG_DEV + agg_ref[...]
    rows = lax.broadcasted_iota(jnp.int32, (8 * n_space, 128), 0)
    wanted = (rows >> 3) * AGG_DEV + (rows & (AGG_DEV - 1))
    named = targets == wanted
    width = VECTORS * VECTORS
    total = jnp.zeros((8 * n_space, width), F32)
    for half in range(2):
        select = jnp.where(named & (((rows >> 2) & 1) == half), 1.0, 0.0).astype(BF16)
        block = pairs[6 * half : 6 * half + 6].reshape(width, 128)
        large = block.astype(BF16)
        rest = block - large.astype(F32)
        middle = rest.astype(BF16)
        small = (rest - middle.astype(F32)).astype(BF16)
        for piece in (large, middle, small):
            total = total + lax.dot_general(
                select, piece, (((1,), (1,)), ((), ())), preferred_element_type=F32)
    terms_out[:, :, 0:width] = (total * (1.0 / (12.0 * BLOCK_SITES))).reshape(n_space, 8, width)
    terms_out[:, :, width:] = jnp.zeros((n_space, 8, LANES - width), F32)

    def term(peer, slot):
        return pltpu.make_async_remote_copy(
            src_ref=terms_out.at[peer], dst_ref=terms_in.at[slot],
            send_sem=term_send.at[peer], recv_sem=term_recv.at[slot],
            device_id=(part, peer), device_id_type=MESH)

    @pl.loop(1, n_space)
    def _(step):
        term(lax.rem(me + step, n_space), me).start()

    coarse_ref[...] = terms_out[me]

    @pl.loop(1, n_space)
    def _(step):
        peer = lax.rem(me + step, n_space)
        term(peer, peer).wait_recv()
        coarse_ref[...] += terms_in[peer]

    @pl.loop(1, n_space)
    def _(step):
        term(lax.rem(me + step, n_space), me).wait_send()

    for chunk in range(CHUNKS):
        for copy in halo(chunk):
            copy.wait_send()


def body(n_space, vectors, links, clover, block_owner, block_aggregate):
    v = vectors.reshape(2, VECTORS, 96, 128)
    u = links.reshape(2, 288, 128)
    c = clover.reshape(2, 576, 128)
    owner = block_owner.reshape(1, 128)
    aggregate = block_aggregate.reshape(1, 128)
    half = (VECTORS, 96, 128)
    applied, coarse = pl.pallas_call(
        functools.partial(kernel, n_space),
        out_shape=(
            jax.ShapeDtypeStruct(v.shape, BF16),
            jax.ShapeDtypeStruct((8, LANES), F32),
        ),
        in_specs=[pl.BlockSpec(memory_space=pltpu.VMEM)] * 5,
        out_specs=(pl.BlockSpec(memory_space=pltpu.VMEM),) * 2,
        scratch_shapes=[
            pltpu.VMEM((2, VECTORS, 12, 8, 128), F32),
            pltpu.VMEM((2, 36, 8, 128), F32),
            pltpu.VMEM((2, 72, 8, 128), F32),
            pltpu.VMEM((2, VECTORS, 12, 8, 128), F32),
            pltpu.VMEM(half, BF16),
            pltpu.VMEM(half, BF16),
            pltpu.VMEM(half, BF16),
            pltpu.VMEM(half, BF16),
            pltpu.VMEM((VECTORS, 24, 128), F32),
            pltpu.VMEM((n_space, 8, LANES), F32),
            pltpu.VMEM((n_space, 8, LANES), F32),
            pltpu.SemaphoreType.DMA((CHUNKS,)),
            pltpu.SemaphoreType.DMA((CHUNKS,)),
            pltpu.SemaphoreType.DMA((CHUNKS,)),
            pltpu.SemaphoreType.DMA((CHUNKS,)),
            pltpu.SemaphoreType.DMA((n_space,)),
            pltpu.SemaphoreType.DMA((n_space,)),
        ],
        compiler_params=pltpu.CompilerParams(
            collective_id=0, has_side_effects=True, vmem_limit_bytes=32 * 1024 * 1024
        ),
    )(v, u, c, owner, aggregate)
    coarse = coarse[:, : VECTORS * VECTORS].reshape(2, AGG_DEV, 6, 2, VECTORS)
    coarse = jnp.transpose(coarse, (1, 3, 4, 0, 2)).reshape(AGG_DEV, 2, VECTORS, VECTORS)
    return (applied.reshape(vectors.shape), coarse)


def solution(mesh):
    return jax.shard_map(
        functools.partial(body, mesh.shape["space"]),
        mesh=mesh,
        in_specs=(
            P(None, None, None, None, ("parts", "space"), None, None),
            P(None, None, None, None, ("parts", "space"), None, None),
            P(None, None, None, None, ("parts", "space"), None, None),
            P(("parts", "space"), None),
            P(("parts", "space")),
        ),
        out_specs=(
            P(None, None, None, None, ("parts", "space"), None, None),
            P(("parts", "space"), None, None, None),
        ),
        check_vma=False,
    )
```

```python
import functools
import jax
import jax.numpy as jnp
from jax import lax
from jax.experimental import pallas as pl
from jax.experimental.pallas import tpu as pltpu
from jax.sharding import PartitionSpec as P

VECTORS = 12
CT = 16
AGG_DEV = 4
BLOCK_SITES = 8
CHUNK = 2
CHUNKS = VECTORS // CHUNK
WIDTH = 96
MESH = pl.DeviceIdType.MESH
F32 = jnp.float32
BF16 = jnp.bfloat16

BACK = (
    ((1, (0, 1)), (0, (0, 1))),
    ((1, (1, 0)), (0, (-1, 0))),
    ((0, (0, 1)), (1, (0, -1))),
    ((0, (1, 0)), (1, (1, 0))),
)


def plus(base, factor, value):
    real, imag = factor
    if real:
        if real > 0:
            return (base[0] + value[0], base[1] + value[1])
        return (base[0] - value[0], base[1] - value[1])
    if imag > 0:
        return (base[0] - value[1], base[1] + value[0])
    return (base[0] + value[1], base[1] - value[0])


def flip(factor):
    return (-factor[0], -factor[1])


def project(mu, sign, field):
    out = []
    for row in range(2):
        column, factor = BACK[mu][row]
        if (sign > 0) != (mu == 3):
            factor = flip(factor)
        out.append([plus(field[row][a], factor, field[2 + column][a]) for a in range(3)])
    return out


def rebuild(mu, sign, total, half):
    for row in range(2):
        for a in range(3):
            total[row][a] = plus(total[row][a], (1, 0), half[row][a])
        column, factor = BACK[mu][row]
        if sign < 0:
            factor = flip(factor)
        for a in range(3):
            total[2 + row][a] = plus(total[2 + row][a], factor, half[column][a])
    return total


def color(link, dagger, half):
    out = []
    for row in half:
        line = []
        for a in range(3):
            real = imag = None
            for b in range(3):
                fr, fi = row[b]
                if dagger:
                    ur, ui = link(b, a)
                    r, i = ur * fr + ui * fi, ur * fi - ui * fr
                else:
                    ur, ui = link(a, b)
                    r, i = ur * fr - ui * fi, ur * fi + ui * fr
                real = r if real is None else real + r
                imag = i if imag is None else imag + i
            line.append((real, imag))
        out.append(line)
    return out


def rounded(half):
    flat = [part for row in half for pair in row for part in pair]
    flat = [part.astype(BF16).astype(F32) for part in flat]
    return unflatten(flat)


def unflatten(flat):
    return [[(flat[(s * 3 + a) * 2], flat[(s * 3 + a) * 2 + 1]) for a in range(3)] for s in range(len(flat) // 6)]


def mapped(half, function):
    return [[(function(p[0]), function(p[1])) for p in row] for row in half]


def rows_of(block, count):
    return [block[8 * i : 8 * i + 8] for i in range(count)]


def gathered(values, level=4):
    if len(values) == 1:
        return values[0]
    low = (lax.broadcasted_iota(jnp.int32, values[0].shape, 0) & level) == 0
    half = len(values) // 2
    out = []
    for i in range(half):
        a, b = values[i], values[i + half]
        kept = jnp.where(low, a, b)
        other = jnp.where(low, b, a)
        if level == 4:
            moved = pltpu.roll(other, 4, axis=0)
        else:
            moved = jnp.where(low, pltpu.roll(other, 8 - level, axis=0), pltpu.roll(other, level, axis=0))
        out.append(kept + moved)
    return gathered(out, level // 2)


def kernel(
    n_space, v_hbm, u_hbm, c_hbm, owner_hbm, agg_hbm, applied_ref, coarse_ref,
    v_ref, u_ref, c_ref, owner_ref, agg_ref, vf, uf, cf, acc, low_out, high_out, low_in, high_in, pairs, terms, terms_out, terms_in,
    v_sem, u_sem, c_sem, owner_sem, agg_sem,
    low_send, low_recv, high_send, high_recv, term_send, term_recv,
):
    part = lax.axis_index("parts")
    me = lax.axis_index("space")
    above = lax.rem(me + 1, n_space)
    below = lax.rem(me + n_space - 1, n_space)
    barrier = pltpu.get_barrier_semaphore()

    u_load = pltpu.make_async_copy(u_hbm, u_ref, u_sem)
    c_load = pltpu.make_async_copy(c_hbm, c_ref, c_sem)
    owner_load = pltpu.make_async_copy(owner_hbm, owner_ref, owner_sem)
    agg_load = pltpu.make_async_copy(agg_hbm, agg_ref, agg_sem)
    v_loads = [
        pltpu.make_async_copy(
            v_hbm.at[:, pl.ds(chunk * CHUNK, CHUNK)], v_ref.at[:, pl.ds(chunk * CHUNK, CHUNK)], v_sem.at[chunk])
        for chunk in range(CHUNKS)
    ]
    u_load.start()
    for load in v_loads:
        load.start()
    c_load.start()
    owner_load.start()
    agg_load.start()

    @pl.loop(1, n_space)
    def _(step):
        peer = lax.rem(me + step, n_space)
        pl.semaphore_signal(barrier, inc=1, device_id=(part, peer), device_id_type=MESH)

    lanes = lax.broadcasted_iota(jnp.int32, (8, 128), 1)
    last_time = (lanes & (CT - 1)) == CT - 1
    first_time = (lanes & (CT - 1)) == 0

    def unpack_links(begin, end):
        for c, i in [(c, i) for c in range(2) for i in range(begin, end)]:
            for j, block in enumerate(rows_of(u_ref[c, 16 * i : 16 * i + 16, :].astype(F32), 2)):
                at = 2 * i + j
                if at >= 27:
                    block = jnp.where(last_time, -block, block)
                uf[c, at] = block

    u_load.wait()
    unpack_links(0, 5)

    def link(mu):
        return lambda a, b: (uf[0, mu * 9 + a * 3 + b], uf[1, mu * 9 + a * 3 + b])

    def field_of(k):
        return [[(vf[0, k, s * 3 + a], vf[1, k, s * 3 + a]) for a in range(3)] for s in range(4)]

    def put_half(ref, k, half):
        flat = [half[s][a][c] for c in range(2) for s in range(2) for a in range(3)]
        for i in range(6):
            both = jnp.concatenate([flat[2 * i], flat[2 * i + 1]], axis=0)
            ref[k, 16 * i : 16 * i + 16, :] = both.astype(BF16)

    def get_half(ref, k):
        flat = []
        for i in range(6):
            flat += rows_of(ref[k, 16 * i : 16 * i + 16, :].astype(F32), 2)
        return [[(flat[s * 3 + a], flat[6 + s * 3 + a]) for a in range(3)] for s in range(2)]

    def halo(chunk):
        at = pl.ds(chunk * CHUNK, CHUNK)
        down = pltpu.make_async_remote_copy(
            src_ref=low_out.at[at], dst_ref=low_in.at[at],
            send_sem=low_send.at[chunk], recv_sem=low_recv.at[chunk],
            device_id=(part, below), device_id_type=MESH)
        up = pltpu.make_async_remote_copy(
            src_ref=high_out.at[at], dst_ref=high_in.at[at],
            send_sem=high_send.at[chunk], recv_sem=high_recv.at[chunk],
            device_id=(part, above), device_id_type=MESH)
        return down, up

    def first(k):
        for c in range(2):
            for i in range(6):
                for j, block in enumerate(rows_of(v_ref[c, k, 16 * i : 16 * i + 16, :].astype(F32), 2)):
                    vf[c, k, 2 * i + j] = block
        field = field_of(k)
        put_half(low_out, k, project(0, -1, field))
        put_half(high_out, k, color(link(0), True, project(0, 1, field)))

    def first_chunk(chunk):
        @pl.loop(0, CHUNK)
        def _(i):
            first(chunk * CHUNK + i)

    for chunk in range(CHUNKS):
        v_loads[chunk].wait()
        first_chunk(chunk)
        if chunk == 0:
            pl.semaphore_wait(barrier, n_space - 1)
        for copy in halo(chunk):
            copy.start()

    unpack_links(5, 18)
    c_load.wait()
    for c in range(2):
        for i in range(36):
            for j, block in enumerate(rows_of(c_ref[c, 16 * i : 16 * i + 16, :].astype(F32), 2)):
                cf[c, 2 * i + j] = block

    def ahead(mu, x):
        if mu == 1:
            return pltpu.roll(x, 7, axis=0)
        if mu == 2:
            return pltpu.roll(x, 128 - CT, axis=1)
        return jnp.where(last_time, pltpu.roll(x, CT - 1, axis=1), pltpu.roll(x, 127, axis=1))

    def behind(mu, x):
        if mu == 1:
            return pltpu.roll(x, 1, axis=0)
        if mu == 2:
            return pltpu.roll(x, CT, axis=1)
        return jnp.where(first_time, pltpu.roll(x, 128 - CT + 1, axis=1), pltpu.roll(x, 1, axis=1))

    @pl.loop(0, VECTORS)
    def _(k):
        total = None
        for mu in range(1, 4):
            field = field_of(k)
            lowered = mapped(rounded(project(mu, -1, field)), functools.partial(ahead, mu))
            forward = color(link(mu), False, lowered)
            raised = rounded(color(link(mu), True, project(mu, 1, field)))
            backward = mapped(raised, functools.partial(behind, mu))
            if total is None:
                zero = jnp.zeros((8, 128), F32)
                total = [[(zero, zero) for _ in range(3)] for _ in range(4)]
            total = rebuild(mu, -1, total, forward)
            total = rebuild(mu, 1, total, backward)
        field = field_of(k)
        for h in range(2):
            for row in range(6):
                real = imag = None
                for column in range(6):
                    at = h * 36 + row * 6 + column
                    cr, ci = cf[0, at], cf[1, at]
                    fr, fi = field[2 * h + column // 3][column % 3]
                    r, i = cr * fr - ci * fi, cr * fi + ci * fr
                    real = r if real is None else real + r
                    imag = i if imag is None else imag + i
                s, a = 2 * h + row // 3, row % 3
                fr, fi = field[s][a]
                tr, ti = total[s][a]
                acc[0, k, s * 3 + a] = 4.0 * fr + real - 0.5 * tr
                acc[1, k, s * 3 + a] = 4.0 * fi + imag - 0.5 * ti

    def finish(j):
        forward = color(link(0), False, get_half(low_in, j))
        backward = get_half(high_in, j)
        zero = jnp.zeros((8, 128), F32)
        total = [[(zero, zero) for _ in range(3)] for _ in range(4)]
        total = rebuild(0, -1, total, forward)
        total = rebuild(0, 1, total, backward)
        right = [[], []]
        for c in range(2):
            for i in range(6):
                both = []
                for at in (2 * i, 2 * i + 1):
                    both.append(acc[c, j, at] - 0.5 * total[at // 3][at % 3][c])
                both = jnp.concatenate(both, axis=0).astype(BF16)
                applied_ref[c, j, 16 * i : 16 * i + 16, :] = both
                right[c] += rows_of(both.astype(F32), 2)
        sums = [[], []]
        for k in range(VECTORS):
            real = imag = None
            for at in range(12):
                vr, vi = vf[0, k, at], vf[1, k, at]
                ar, ai = right[0][at], right[1][at]
                r, i = vr * ar + vi * ai, vr * ai - vi * ar
                real = r if real is None else real + r
                imag = i if imag is None else imag + i
            sums[0].append(real)
            sums[1].append(imag)
        flat = sums[0] + sums[1]
        for g in range(3):
            pairs[j, 8 * g : 8 * g + 8, :] = gathered(flat[8 * g : 8 * g + 8])

    owner_load.wait()
    agg_load.wait()
    targets = owner_ref[...] * AGG_DEV + agg_ref[...]
    rows = lax.broadcasted_iota(jnp.int32, (16 * n_space, 128), 0)
    named = targets == (rows >> 4) * AGG_DEV + (rows & (AGG_DEV - 1))
    group = (rows >> 2) & 3

    def reduce(g):
        select = jnp.where(named & (group == g), 1.0, 0.0).astype(BF16)
        block = pairs[4 * g : 4 * g + 4].reshape(WIDTH, 128)
        large = block.astype(BF16)
        rest = block - large.astype(F32)
        middle = rest.astype(BF16)
        small = (rest - middle.astype(F32)).astype(BF16)
        total = None
        for piece in (large, middle, small):
            product = lax.dot_general(
                select, piece, (((1,), (1,)), ((), ())), preferred_element_type=F32)
            total = product if total is None else total + product
        return total

    terms[:, WIDTH:] = jnp.zeros((16 * n_space, 128 - WIDTH), F32)
    for chunk in range(CHUNKS):
        for copy in halo(chunk):
            copy.wait_recv()

        @pl.loop(0, CHUNK)
        def _(i, chunk=chunk):
            finish(chunk * CHUNK + i)

        done = (chunk + 1) * CHUNK
        if done % 4 == 0:
            if done == 4:
                terms[:, 0:WIDTH] = reduce(0)
            else:
                terms[:, 0:WIDTH] += reduce(done // 4 - 1)
    terms_out[...] = terms[...].astype(BF16).reshape(n_space, 16, 128)

    def term(peer, slot):
        return pltpu.make_async_remote_copy(
            src_ref=terms_out.at[peer], dst_ref=terms_in.at[slot],
            send_sem=term_send.at[peer], recv_sem=term_recv.at[slot],
            device_id=(part, peer), device_id_type=MESH)

    @pl.loop(1, n_space)
    def _(step):
        term(lax.rem(me + step, n_space), me).start()

    mine = terms[pl.ds(pl.multiple_of(me * 16, 16), 16), :]
    coarse_ref[...] = mine

    @pl.loop(1, n_space)
    def _(step):
        peer = lax.rem(me + step, n_space)
        term(peer, peer).wait_recv()
        coarse_ref[...] += terms_in[peer].astype(F32)

    @pl.loop(1, n_space)
    def _(step):
        term(lax.rem(me + step, n_space), me).wait_send()

    coarse_ref[...] *= 1.0 / (12.0 * BLOCK_SITES)

    for chunk in range(CHUNKS):
        for copy in halo(chunk):
            copy.wait_send()


def body(n_space, vectors, links, clover, block_owner, block_aggregate):
    v = vectors.reshape(2, VECTORS, 96, 128)
    u = links.reshape(2, 288, 128)
    c = clover.reshape(2, 576, 128)
    owner = block_owner.reshape(1, 128)
    aggregate = block_aggregate.reshape(1, 128)
    v, u, c, owner, aggregate = [
        pltpu.with_memory_space_constraint(x, pltpu.HBM) for x in (v, u, c, owner, aggregate)]
    half = (VECTORS, 96, 128)
    applied, coarse = pl.pallas_call(
        functools.partial(kernel, n_space),
        out_shape=(
            jax.ShapeDtypeStruct(v.shape, BF16),
            jax.ShapeDtypeStruct((16, 128), F32),
        ),
        in_specs=[pl.BlockSpec(memory_space=pltpu.HBM)] * 5,
        out_specs=(pl.BlockSpec(memory_space=pltpu.VMEM),) * 2,
        scratch_shapes=[
            pltpu.VMEM(v.shape, BF16),
            pltpu.VMEM(u.shape, BF16),
            pltpu.VMEM(c.shape, BF16),
            pltpu.VMEM((1, 128), jnp.int32),
            pltpu.VMEM((1, 128), jnp.int32),
            pltpu.VMEM((2, VECTORS, 12, 8, 128), F32),
            pltpu.VMEM((2, 36, 8, 128), F32),
            pltpu.VMEM((2, 72, 8, 128), F32),
            pltpu.VMEM((2, VECTORS, 12, 8, 128), F32),
            pltpu.VMEM(half, BF16),
            pltpu.VMEM(half, BF16),
            pltpu.VMEM(half, BF16),
            pltpu.VMEM(half, BF16),
            pltpu.VMEM((VECTORS, 24, 128), F32),
            pltpu.VMEM((16 * n_space, 128), F32),
            pltpu.VMEM((n_space, 16, 128), BF16),
            pltpu.VMEM((n_space, 16, 128), BF16),
            pltpu.SemaphoreType.DMA((CHUNKS,)),
            pltpu.SemaphoreType.DMA,
            pltpu.SemaphoreType.DMA,
            pltpu.SemaphoreType.DMA,
            pltpu.SemaphoreType.DMA,
            pltpu.SemaphoreType.DMA((CHUNKS,)),
            pltpu.SemaphoreType.DMA((CHUNKS,)),
            pltpu.SemaphoreType.DMA((CHUNKS,)),
            pltpu.SemaphoreType.DMA((CHUNKS,)),
            pltpu.SemaphoreType.DMA((n_space,)),
            pltpu.SemaphoreType.DMA((n_space,)),
        ],
        compiler_params=pltpu.CompilerParams(
            collective_id=0, has_side_effects=True, vmem_limit_bytes=32 * 1024 * 1024
        ),
    )(v, u, c, owner, aggregate)
    coarse = coarse[:12, :WIDTH].reshape(3, AGG_DEV, 4, 2, VECTORS)
    coarse = jnp.transpose(coarse, (1, 3, 4, 0, 2)).reshape(AGG_DEV, 2, VECTORS, VECTORS)
    return (applied.reshape(vectors.shape), coarse)


def solution(mesh):
    return jax.shard_map(
        functools.partial(body, mesh.shape["space"]),
        mesh=mesh,
        in_specs=(
            P(None, None, None, None, ("parts", "space"), None, None),
            P(None, None, None, None, ("parts", "space"), None, None),
            P(None, None, None, None, ("parts", "space"), None, None),
            P(("parts", "space"), None),
            P(("parts", "space")),
        ),
        out_specs=(
            P(None, None, None, None, ("parts", "space"), None, None),
            P(("parts", "space"), None, None, None),
        ),
        check_vma=False,
    )
```
